256 devices in a mesh: va: 8 (over z_hi, y), vb: 4 (over z_lo), oj: 8 (over x, core).
Axes of the slice: x: 4, y: 4, z: 8 (z_hi: 2, z_lo: 4; z = z_hi * 4 + z_lo), core: 2. Of those that a mesh axis runs over, the one named last changes fastest.
Arguments:
- occ_slab: bfloat16 [3584, 2, 2048], P(('vb', 'oj'), None, 'va'), may hold values from -0.875 to 0.875
- pair_slab: bfloat16 [3584, 8, 2048], P(('va', 'oj'), None, 'vb'), may hold values from -0.875 to 0.875
- occ_energy: float32 [2], replicated, may hold values from -1.5 to -0.3
- pair_energy: float32 [8], P('oj'), may hold values from -1.5 to -0.3
- vir_energy: float32 [2048], replicated, may hold values from 0.2 to 3
Outputs:
- gamma_occ: float32 [3584, 2, 2048], P(('vb', 'oj'), None, 'va')
- gamma_pair: float32 [3584, 8, 2048], P('va', 'oj', 'vb')
The draws below stay inside these ranges and needn't reach their ends.
All inputs are finite; a program needn't handle non-finite values.
Results may differ from the reference program's by a relative error of at most 0.002.
Values may be sent and summed in bfloat16 or wider, within the bound.
A program may use at most 128 MiB of HBM per device.

```python
import math
import jax
import jax.numpy as jnp
from jax import lax

V = 2048
NAUX = 3584
NI = 2
NJ = 8


def steps_of(own_key, shape, pieces, least, top_value):
    def one(axis_at, parts):
        steps = jax.random.uniform(jax.random.fold_in(jax.random.fold_in(own_key, 6), axis_at), (parts,), jnp.float32, least / len(pieces), top_value / len(pieces))
        return jnp.repeat(jnp.exp(steps), shape[axis_at] // parts).reshape((-1,) + (1,) * (len(shape) - axis_at - 1))

    gain = one(*pieces[0])
    for cut in pieces[1:]:
        gain = gain * one(*cut)
    return gain


def normal_values(own_key, shape, spread, bound, pieces=(), held_as=jnp.bfloat16):
    gain = steps_of(own_key, shape, pieces, -0.22, 0.18) if pieces else 1.0
    values = jax.random.normal(own_key, shape, jnp.float32) * spread * gain
    return jnp.minimum(jnp.maximum(values, -bound), bound).astype(held_as)


def setup_inputs(seed: int = 0) -> dict:
    streams_of = jax.random.split(jax.random.key(seed), 6)
    occ_slab = normal_values(streams_of[0], (NAUX, NI, V), (1.5 * (NJ * V) ** -0.333), 0.875, ((0, 32), (2, 8)))
    pair_slab = normal_values(streams_of[1], (NAUX, NJ, V), (1.5 * (NJ * V) ** -0.333), 0.875, ((0, 64), (2, 4)))
    occ_energy = jnp.clip(jax.random.uniform(streams_of[2], (NI,), jnp.float32, -1.5, -0.3), -1.5, -0.3)
    pair_energy = jnp.clip(-1.5 + 1.2 * jax.random.uniform(streams_of[3], (NJ,), jnp.float32) ** steps_of(streams_of[3], (NJ,), ((0, 8),), -0.2, 0.2), -1.5, -0.3)
    vir_energy = jnp.clip(jnp.exp(jax.random.uniform(streams_of[4], (V,), jnp.float32, math.log(0.2), math.log(3.0))), 0.2, 3.0)
    return {"occ_slab": occ_slab, "pair_slab": pair_slab, "occ_energy": occ_energy, "pair_energy": pair_energy, "vir_energy": vir_energy}


def reference(occ_slab, pair_slab, occ_energy, pair_energy, vir_energy):
    occ_wide = occ_slab.astype(jnp.float32)

    def one_pair(running, index):
        pair_rows = lax.dynamic_index_in_dim(pair_slab, index, 1, keepdims=False).astype(jnp.float32)
        pair_ints = jnp.einsum('qia,qb->iab', occ_wide, pair_rows)
        energy_j = lax.dynamic_index_in_dim(pair_energy, index, 0, keepdims=False)
        denominator = ((occ_energy[:, None, None] + energy_j) - vir_energy[None, :, None]) - vir_energy[None, None, :]
        amplitudes = (pair_ints / denominator).astype(jnp.bfloat16).astype(jnp.float32)
        gamma_part = jnp.einsum('iab,qb->qia', amplitudes, pair_rows)
        gamma_column = jnp.einsum('iab,qia->qb', amplitudes, occ_wide)
        return running + gamma_part, gamma_column

    initial = jnp.zeros((NAUX, NI, V), jnp.float32)
    gamma_occ, columns = lax.scan(one_pair, initial, jnp.arange(NJ, dtype=jnp.int32))
    gamma_pair = jnp.transpose(columns, (1, 0, 2))
    return gamma_occ, gamma_pair
```

```python
import jax
import jax.numpy as jnp
from jax import lax
from jax.experimental import pallas as pl
from jax.experimental.pallas import tpu as pltpu
from jax.sharding import PartitionSpec as P

MESH = pl.DeviceIdType.MESH
BF = jnp.bfloat16
F32 = jnp.float32
ORDER = (0, 1, 3, 2)
PLUS = (0, 3)


def dot(a, b, ca, cb):
    return lax.dot_general(a, b, (((ca,), (cb,)), ((), ())), preferred_element_type=F32)


class Sems:
    def __init__(self, ref, count):
        self.ref, self.count, self.names = ref, count, {}

    def __getitem__(self, name):
        at = self.names.setdefault(name, len(self.names))
        assert at < self.count
        return self.ref.at[at]


N_SEMS = 160


def kernel(
    occ_ref, pair_ref, eo_ref, ep_ref, vir_ref,
    go_ref, gp_ref,
    stage, pairs, zrelay, occs, ecol, tacc, tb,
    gpf, gps, gr, gl, gf, zs2, zr2,
    hof, hsib, hsibr, hxs, hr, hl, hf, hz,
    send_sem, recv_sem,
):
    va, vb, oj = lax.axis_index("va"), lax.axis_index("vb"), lax.axis_index("oj")
    zh, y = va // 4, va % 4
    x, c = oj // 2, oj % 2
    other_c = 1 - c
    z = zh * 4 + vb
    ssem, rsem = Sems(send_sem, N_SEMS), Sems(recv_sem, N_SEMS)
    started = []

    def at_x(dx, dc=False):
        return {"oj": ((x + dx) % 4) * 2 + (other_c if dc else c)}

    def at_y(dy):
        return {"va": zh * 4 + (y + dy) % 4}

    def at_vb(dz):
        return {"vb": (vb + dz) % 4}

    def at_z(zz):
        zz = zz % 8
        return {"va": (zz // 4) * 4 + y, "vb": zz % 4}

    up2 = z + 2 - 4 * c + 8
    up2_dev = at_z(up2)
    down2_dev = at_z(z - 2 + 4 * c + 8)

    def send(name, src, dst, dev):
        copy = pltpu.make_async_remote_copy(
            src_ref=src, dst_ref=dst, send_sem=ssem[name], recv_sem=rsem[name],
            device_id=dev, device_id_type=MESH,
        )
        copy.start()
        started.append(copy)

    def arrived(name, dst):
        pltpu.make_async_remote_copy(
            src_ref=dst, dst_ref=dst, send_sem=ssem[name], recv_sem=rsem[name],
            device_id=at_x(0, True), device_id_type=MESH,
        ).wait_recv()

    barrier = pltpu.get_barrier_semaphore()
    partners = [at_x(dx, dc) for dx in range(4) for dc in (False, True) if dx or dc]
    partners += [at_vb(1), at_vb(2), at_vb(3), at_y(1), at_y(3), up2_dev, down2_dev]
    for dev in partners:
        pl.semaphore_signal(barrier, inc=1, device_id=dev, device_id_type=MESH)
    pl.semaphore_wait(barrier, len(partners))

    def pblk(h, yy, xx):
        hh = zh if h == 0 else 1 - zh
        return pairs.at[(hh * 4 + yy) * 2 + xx // 2, xx % 2]

    def xs(e):
        return (x + 4 - e) % 4

    def zsrc(f):
        return (vb + 4 - f) % 4

    def oblk(f, dx, sib=False):
        return occs.at[zsrc(f) * 8 + ((x + dx) % 4) * 2 + (other_c if sib else c)]

    for dx, dc in ((0, True), (1, False), (1, True), (3, False), (3, True), (2, False), (2, True)):
        dev = at_x(dx, dc)
        send(("s1", dx, dc), pair_ref.at[dev["oj"]], stage.at[dx * 2 + int(dc)], dev)
    own_rows = occs.at[vb * 8 + oj]
    for f in (1, 3, 2):
        send(("oz", f), occ_ref, own_rows, at_vb(f))
    own_rows[...] = occ_ref[...]
    stage[0] = pair_ref[oj]

    def occ_spread(f):
        blk = oblk(f, 0)
        send(("oR", f), blk, blk, at_x(1))
        send(("oL", f), blk, blk, at_x(3))
        send(("oS", 0, f), blk, blk, at_x(0, True))

    def pair_merge(e):
        if e == 0:
            arrived(("s1", 0, True), stage.at[1])
        else:
            for dc in (False, True):
                arrived(("s1", e, dc), stage.at[e * 2 + int(dc)])
        low = stage[e * 2 + c].astype(F32)
        high = stage[e * 2 + other_c].astype(F32)
        blk = pblk(0, y, xs(e))
        blk[...] = jnp.concatenate([low, high], axis=0).astype(BF)
        send(("zr", e), blk, zrelay.at[e], up2_dev)
        pair_spread(0, e)

    def pair_spread(h, e):
        blk = pblk(h, y, xs(e))
        send(("yR", h, e), blk, blk, at_y(1))
        send(("yL", h, e), blk, blk, at_y(3))

    pair_merge(0)
    occ_spread(0)
    pair_merge(1)
    pair_merge(3)
    pair_merge(2)

    va_row = vir_ref[:, pl.ds(pl.multiple_of(va * 256, 256), 256)]
    ecol[...] = jnp.broadcast_to(va_row, (128, 256)).T
    tacc[...] = jnp.zeros_like(tacc)

    for f in (1, 3, 2):
        arrived(("oz", f), oblk(f, 0))
        occ_spread(f)

    zorig = ((z - 2 + 4 * c + 8) % 8) // 4

    def z_forward(e):
        arrived(("zr", e), zrelay.at[e])
        dst = pairs.at[(zorig * 4 + y) * 2 + xs(e) // 2, xs(e) % 2]
        send(("zf", e), zrelay.at[e], dst, up2_dev)

    def y_forward(h, e):
        right = pblk(h, (y + 3) % 4, xs(e))
        left = pblk(h, (y + 1) % 4, xs(e))
        if e in PLUS:
            arrived(("yR", h, e), right)
            send(("yF", h, e), right, right, at_y(1))
            arrived(("yL", h, e), left)
        else:
            arrived(("yL", h, e), left)
            send(("yF", h, e), left, left, at_y(3))
            arrived(("yR", h, e), right)

    def occ_forward(f):
        right, left = oblk(f, 3), oblk(f, 1)
        arrived(("oR", f), right)
        if f in PLUS:
            send(("oF", f), right, right, at_x(1))
        send(("oS", 1, f), right, right, at_x(0, True))
        arrived(("oL", f), left)
        if f not in PLUS:
            send(("oF", f), left, left, at_x(3))
        send(("oS", 2, f), left, left, at_x(0, True))

    for e in ORDER:
        z_forward(e)
        y_forward(0, e)
        occ_forward(e)
    for e in ORDER:
        arrived(("zf", e), pblk(1, y, xs(e)))
        pair_spread(1, e)
    for f in ORDER:
        far = oblk(f, 2)
        arrived(("oF", f), far)
        send(("oS", 3, f), far, far, at_x(0, True))
    for f in ORDER:
        for m, dx in ((0, 0), (1, 3), (2, 1), (3, 2)):
            arrived(("oS", m, f), oblk(f, dx, True))

    def t_add(h, dy):
        hh = zh if h == 0 else 1 - zh
        group = hh * 4 + (y + dy) % 4
        a = occs[pl.ds(group * 4, 4)].reshape(448, 512)
        b = pairs[pl.ds(group * 2, 2)].reshape(448, 512)
        tacc[...] += dot(a, b, 0, 0)

    t_add(0, 0)
    t_add(0, 1)
    t_add(0, 3)
    t_add(1, 0)
    for e in ORDER:
        y_forward(1, e)
    t_add(1, 1)
    t_add(1, 3)
    for e in ORDER:
        arrived(("yF", 0, e), pblk(0, (y + 2) % 4, xs(e)))
    t_add(0, 2)
    for e in ORDER:
        arrived(("yF", 1, e), pblk(1, (y + 2) % 4, xs(e)))
    t_add(1, 2)

    vb_row = vir_ref[:, pl.ds(pl.multiple_of(vb * 512, 512), 512)]
    va_cols = jnp.concatenate([ecol[...]] * 4, axis=1)
    for i in range(2):
        den = ((eo_ref[i] + ep_ref[0]) - va_cols) - vb_row
        tb[i * 256:(i + 1) * 256] = (tacc[i * 256:(i + 1) * 256] / den).astype(BF)

    def g_block(h, dy):
        hh = zh if h == 0 else 1 - zh
        group = hh * 4 + (y + dy) % 4
        rows = occs[pl.ds(group * 4, 4)].reshape(448, 512)
        gpf[h, dy] = dot(rows, tb[...], 1, 0).reshape(4, 112, 512)

    def g_direct(h, dy, t, name, dev, dst):
        gps[h, dy, t] = gpf[h, dy, t].astype(BF)
        send((name, h, t), gps.at[h, dy, t], dst.at[h, t], dev)

    def g_start(h):
        g_block(h, 2)
        for t in range(4):
            g_direct(h, 2, t, "gF", at_y(1 if t in PLUS else 3), gf)
        g_block(h, 1)
        g_block(h, 3)
        for t in range(4):
            if t in PLUS:
                g_direct(h, 3, t, "gL", at_y(3), gl)
            else:
                g_direct(h, 1, t, "gR", at_y(1), gr)

    def g_relay(h):
        for t in range(4):
            arrived(("gF", h, t), gf.at[h, t])
            dy = 1 if t in PLUS else 3
            gps[h, dy, t] = (gpf[h, dy, t] + gf[h, t].astype(F32)).astype(BF)
            if t in PLUS:
                send(("gR", h, t), gps.at[h, dy, t], gr.at[h, t], at_y(1))
            else:
                send(("gL", h, t), gps.at[h, dy, t], gl.at[h, t], at_y(3))

    def g_sum(h, t):
        arrived(("gR", h, t), gr.at[h, t])
        arrived(("gL", h, t), gl.at[h, t])
        return gpf[h, 0, t] + gr[h, t].astype(F32) + gl[h, t].astype(F32)

    def h_block(f):
        group = (vb + f) % 4
        rows = pairs[pl.ds(group * 4, 4), other_c].reshape(448, 512)
        hsib[f] = dot(rows, tb[...], 1, 1).astype(BF).reshape(4, 112, 512)
        send(("hS", f), hsib.at[f], hsibr.at[f], at_x(0, True))
        rows = pairs[pl.ds(group * 4, 4), c].reshape(448, 512)
        hof[f] = dot(rows, tb[...], 1, 1).reshape(4, 112, 512)

    def h_start(f):
        arrived(("hS", f), hsibr.at[f])
        hof[f] += hsibr[f].astype(F32)
        hxs[f, 2] = hof[f, (x + 2) % 4].astype(BF)
        send(("hF", f), hxs.at[f, 2], hf.at[f], at_x(1 if f in PLUS else 3))
        if f in PLUS:
            hxs[f, 3] = hof[f, (x + 3) % 4].astype(BF)
            send(("hL", f), hxs.at[f, 3], hl.at[f], at_x(3))
        else:
            hxs[f, 1] = hof[f, (x + 1) % 4].astype(BF)
            send(("hR", f), hxs.at[f, 1], hr.at[f], at_x(1))

    def h_relay(f):
        arrived(("hF", f), hf.at[f])
        dx = 1 if f in PLUS else 3
        hxs[f, dx] = (hof[f, (x + dx) % 4] + hf[f].astype(F32)).astype(BF)
        if f in PLUS:
            send(("hR", f), hxs.at[f, dx], hr.at[f], at_x(1))
        else:
            send(("hL", f), hxs.at[f, dx], hl.at[f], at_x(3))

    def h_sum(f):
        arrived(("hR", f), hr.at[f])
        arrived(("hL", f), hl.at[f])
        return hof[f, x] + hr[f].astype(F32) + hl[f].astype(F32)

    def h_finish(f):
        hxs[f, 0] = h_sum(f).astype(BF)
        send(("hz", f), hxs.at[f, 0], hz.at[f], at_vb(f))

    g_start(1)
    g_start(0)
    h_block(2)
    h_block(1)
    g_relay(1)
    h_start(2)
    h_start(1)
    h_block(3)
    h_block(0)
    h_start(3)
    h_start(0)
    g_block(1, 0)
    g_block(0, 0)
    h_relay(2)
    h_relay(1)
    h_relay(3)
    h_relay(0)
    for t in range(4):
        gps[1, 0, t] = g_sum(1, t).astype(BF)
        send(("z2", t), gps.at[1, 0, t], zr2.at[t], up2_dev)
    h_finish(2)
    h_finish(1)
    h_finish(3)
    g_relay(0)
    for t in range(4):
        arrived(("z2", t), zr2.at[t])
        send(("z3", t), zr2.at[t], zs2.at[t], up2_dev)
    total = h_sum(0)
    for f in (1, 3, 2):
        arrived(("hz", f), hz.at[f])
        total = total + hz[f].astype(F32)
    go_ref[...] = total
    for t in range(4):
        part = g_sum(0, t)
        arrived(("z3", t), zs2.at[t])
        gp_ref[t] = part + zs2[t].astype(F32)
    for copy in started:
        copy.wait_send()


def per_device(occ_slab, pair_slab, occ_energy, pair_energy, vir_energy):
    vmem = pl.BlockSpec(memory_space=pltpu.VMEM)
    smem = pl.BlockSpec(memory_space=pltpu.SMEM)
    chunk = (112, 512)
    gamma_occ, gamma_pair = pl.pallas_call(
        kernel,
        out_shape=(jax.ShapeDtypeStruct(chunk, F32), jax.ShapeDtypeStruct((4,) + chunk, F32)),
        in_specs=[vmem, vmem, smem, smem, vmem],
        out_specs=(vmem, vmem),
        scratch_shapes=[
            pltpu.VMEM((8, 56, 512), BF),
            pltpu.VMEM((16, 2) + chunk, BF),
            pltpu.VMEM((4,) + chunk, BF),
            pltpu.VMEM((32,) + chunk, BF),
            pltpu.VMEM((256, 128), F32),
            pltpu.VMEM((512, 512), F32),
            pltpu.VMEM((512, 512), BF),
            pltpu.VMEM((2, 4, 4) + chunk, F32),
            pltpu.VMEM((2, 4, 4) + chunk, BF),
            pltpu.VMEM((2, 4) + chunk, BF),
            pltpu.VMEM((2, 4) + chunk, BF),
            pltpu.VMEM((2, 4) + chunk, BF),
            pltpu.VMEM((4,) + chunk, BF),
            pltpu.VMEM((4,) + chunk, BF),
            pltpu.VMEM((4, 4) + chunk, F32),
            pltpu.VMEM((4, 4) + chunk, BF),
            pltpu.VMEM((4, 4) + chunk, BF),
            pltpu.VMEM((4, 4) + chunk, BF),
            pltpu.VMEM((4,) + chunk, BF),
            pltpu.VMEM((4,) + chunk, BF),
            pltpu.VMEM((4,) + chunk, BF),
            pltpu.VMEM((4,) + chunk, BF),
            pltpu.SemaphoreType.DMA((N_SEMS,)),
            pltpu.SemaphoreType.DMA((N_SEMS,)),
        ],
        compiler_params=pltpu.CompilerParams(
            collective_id=0, has_side_effects=True, vmem_limit_bytes=60 * 1024 * 1024
        ),
        cost_estimate=pl.CostEstimate(flops=5_600_000_000, bytes_accessed=2_000_000, transcendentals=0),
    )(
        occ_slab.reshape(chunk),
        jnp.swapaxes(pair_slab, 0, 1),
        occ_energy,
        pair_energy,
        vir_energy.reshape(1, -1),
    )
    return gamma_occ.reshape(112, 2, 256), gamma_pair.reshape(448, 1, 512)


def solution(mesh):
    placed = (P(("vb", "oj"), None, "va"), P(("va", "oj"), None, "vb"), P(), P("oj"), P())
    return jax.shard_map(
        per_device,
        mesh=mesh,
        in_specs=placed,
        out_specs=(P(("vb", "oj"), None, "va"), P("va", "oj", "vb")),
        check_vma=False,
    )
```

```python
import jax
import jax.numpy as jnp
from jax import lax
from jax.experimental import pallas as pl
from jax.experimental.pallas import tpu as pltpu
from jax.sharding import PartitionSpec as P

MESH = pl.DeviceIdType.MESH
BF = jnp.bfloat16
F32 = jnp.float32
ORDER = (0, 1, 3, 2)
PLUS = (0, 3)


def dot(a, b, ca, cb):
    return lax.dot_general(a, b, (((ca,), (cb,)), ((), ())), preferred_element_type=F32)


class Sems:
    def __init__(self, ref, count):
        self.ref, self.count, self.names = ref, count, {}

    def __getitem__(self, name):
        at = self.names.setdefault(name, len(self.names))
        assert at < self.count
        return self.ref.at[at]


N_SEMS = 160


def kernel(
    occ_ref, pair_ref, eo_ref, ep_ref, vir_ref,
    go_ref, gp_ref,
    stage, pairs, zrelay, occs, ecol, tacc, tb,
    gpf, gps, gr, gl, gf, zs2, zr2,
    hof, hsib, hsibr, hxs, hr, hl, hf, hz,
    send_sem, recv_sem,
):
    va, vb, oj = lax.axis_index("va"), lax.axis_index("vb"), lax.axis_index("oj")
    zh, y = va // 4, va % 4
    x, c = oj // 2, oj % 2
    other_c = 1 - c
    z = zh * 4 + vb
    ssem, rsem = Sems(send_sem, N_SEMS), Sems(recv_sem, N_SEMS)
    started = []

    def at_x(dx, dc=False):
        return {"oj": ((x + dx) % 4) * 2 + (other_c if dc else c)}

    def at_y(dy):
        return {"va": zh * 4 + (y + dy) % 4}

    def at_vb(dz):
        return {"vb": (vb + dz) % 4}

    def at_z(zz):
        zz = zz % 8
        return {"va": (zz // 4) * 4 + y, "vb": zz % 4}

    up2 = z + 2 - 4 * c + 8
    up2_dev = at_z(up2)
    down2_dev = at_z(z - 2 + 4 * c + 8)

    def send(name, src, dst, dev):
        copy = pltpu.make_async_remote_copy(
            src_ref=src, dst_ref=dst, send_sem=ssem[name], recv_sem=rsem[name],
            device_id=dev, device_id_type=MESH,
        )
        copy.start()
        started.append(copy)

    def arrived(name, dst):
        pltpu.make_async_remote_copy(
            src_ref=dst, dst_ref=dst, send_sem=ssem[name], recv_sem=rsem[name],
            device_id=at_x(0, True), device_id_type=MESH,
        ).wait_recv()

    barrier = pltpu.get_barrier_semaphore()
    partners = [at_x(dx, dc) for dx in range(4) for dc in (False, True) if dx or dc]
    partners += [at_vb(1), at_vb(2), at_vb(3), at_y(1), at_y(3), up2_dev, down2_dev]
    for dev in partners:
        pl.semaphore_signal(barrier, inc=1, device_id=dev, device_id_type=MESH)
    pl.semaphore_wait(barrier, len(partners))

    def pblk(h, yy, xx):
        hh = zh if h == 0 else 1 - zh
        return pairs.at[(hh * 4 + yy) * 2 + xx // 2, xx % 2]

    def xs(e):
        return (x + 4 - e) % 4

    def zsrc(f):
        return (vb + 4 - f) % 4

    def oblk(f, dx, sib=False):
        return occs.at[zsrc(f) * 8 + ((x + dx) % 4) * 2 + (other_c if sib else c)]

    for dx, dc in ((0, True), (1, False), (1, True), (3, False), (3, True), (2, False), (2, True)):
        dev = at_x(dx, dc)
        send(("s1", dx, dc), pair_ref.at[dev["oj"]], stage.at[dx * 2 + int(dc)], dev)
    own_rows = occs.at[vb * 8 + oj]
    for f in (1, 3, 2):
        send(("oz", f), occ_ref, own_rows, at_vb(f))
    own_rows[...] = occ_ref[...]
    stage[0] = pair_ref[oj]

    def occ_spread(f):
        blk = oblk(f, 0)
        send(("oR", f), blk, blk, at_x(1))
        send(("oL", f), blk, blk, at_x(3))
        send(("oS", 0, f), blk, blk, at_x(0, True))

    def pair_merge(e):
        if e == 0:
            arrived(("s1", 0, True), stage.at[1])
        else:
            for dc in (False, True):
                arrived(("s1", e, dc), stage.at[e * 2 + int(dc)])
        low = stage[e * 2 + c].astype(F32)
        high = stage[e * 2 + other_c].astype(F32)
        blk = pblk(0, y, xs(e))
        blk[...] = jnp.concatenate([low, high], axis=0).astype(BF)
        send(("zr", e), blk, zrelay.at[e], up2_dev)
        pair_spread(0, e)

    def pair_spread(h, e):
        blk = pblk(h, y, xs(e))
        send(("yR", h, e), blk, blk, at_y(1))
        send(("yL", h, e), blk, blk, at_y(3))

    zorig = ((z - 2 + 4 * c + 8) % 8) // 4

    def z_forward(e):
        arrived(("zr", e), zrelay.at[e])
        dst = pairs.at[(zorig * 4 + y) * 2 + xs(e) // 2, xs(e) % 2]
        send(("zf", e), zrelay.at[e], dst, up2_dev)

    def y_forward(h, e):
        right = pblk(h, (y + 3) % 4, xs(e))
        left = pblk(h, (y + 1) % 4, xs(e))
        if e in PLUS:
            arrived(("yR", h, e), right)
            send(("yF", h, e), right, right, at_y(1))
            arrived(("yL", h, e), left)
        else:
            arrived(("yL", h, e), left)
            send(("yF", h, e), left, left, at_y(3))
            arrived(("yR", h, e), right)

    def occ_forward(f):
        right, left = oblk(f, 3), oblk(f, 1)
        arrived(("oR", f), right)
        if f in PLUS:
            send(("oF", f), right, right, at_x(1))
        send(("oS", 1, f), right, right, at_x(0, True))
        arrived(("oL", f), left)
        if f not in PLUS:
            send(("oF", f), left, left, at_x(3))
        send(("oS", 2, f), left, left, at_x(0, True))

    va_row = vir_ref[:, pl.ds(pl.multiple_of(va * 256, 256), 256)]
    ecol[...] = jnp.broadcast_to(va_row, (128, 256)).T
    tacc[...] = jnp.zeros_like(tacc)

    def occ_in(f):
        arrived(("oz", f), oblk(f, 0))
        occ_spread(f)

    def z_in(e):
        arrived(("zf", e), pblk(1, y, xs(e)))
        pair_spread(1, e)

    def occ_far(f):
        far = oblk(f, 2)
        arrived(("oF", f), far)
        send(("oS", 3, f), far, far, at_x(0, True))

    pair_merge(0)
    occ_spread(0)
    pair_merge(1)
    pair_merge(3)
    y_forward(0, 0)
    pair_merge(2)
    z_forward(0)
    y_forward(0, 1)
    occ_in(1)
    y_forward(0, 3)
    z_forward(1)
    occ_in(3)
    y_forward(0, 2)
    z_in(0)
    occ_in(2)
    occ_forward(0)
    z_forward(3)
    occ_forward(1)
    z_in(1)
    y_forward(1, 0)
    z_forward(2)
    occ_forward(3)
    occ_far(0)
    z_in(3)
    y_forward(1, 1)
    occ_forward(2)
    occ_far(1)
    z_in(2)
    y_forward(1, 3)
    occ_far(3)
    occ_far(2)
    y_forward(1, 2)
    for f in ORDER:
        for m, dx in ((0, 0), (1, 3), (2, 1), (3, 2)):
            arrived(("oS", m, f), oblk(f, dx, True))

    def t_add(h, dy):
        hh = zh if h == 0 else 1 - zh
        group = hh * 4 + (y + dy) % 4
        a = occs[pl.ds(group * 4, 4)].reshape(448, 512)
        b = pairs[pl.ds(group * 2, 2)].reshape(448, 512)
        tacc[...] += dot(a, b, 0, 0)

    t_add(0, 0)
    t_add(0, 1)
    t_add(0, 3)
    t_add(1, 0)
    for e in ORDER:
        arrived(("yF", 0, e), pblk(0, (y + 2) % 4, xs(e)))
    t_add(0, 2)
    t_add(1, 1)
    t_add(1, 3)
    for e in ORDER:
        arrived(("yF", 1, e), pblk(1, (y + 2) % 4, xs(e)))
    t_add(1, 2)

    vb_row = vir_ref[:, pl.ds(pl.multiple_of(vb * 512, 512), 512)]
    va_cols = jnp.concatenate([ecol[...]] * 4, axis=1)
    for i in range(2):
        den = ((eo_ref[i] + ep_ref[0]) - va_cols) - vb_row
        tb[i * 256:(i + 1) * 256] = (tacc[i * 256:(i + 1) * 256] / den).astype(BF)

    def g_block(h, dy):
        hh = zh if h == 0 else 1 - zh
        group = hh * 4 + (y + dy) % 4
        rows = occs[pl.ds(group * 4, 4)].reshape(448, 512)
        gpf[h, dy] = dot(rows, tb[...], 1, 0).reshape(4, 112, 512)

    def g_direct(h, dy, t, name, dev, dst):
        gps[h, dy, t] = gpf[h, dy, t].astype(BF)
        send((name, h, t), gps.at[h, dy, t], dst.at[h, t], dev)

    def g_far(h):
        g_block(h, 2)
        for t in range(4):
            g_direct(h, 2, t, "gF", at_y(1 if t in PLUS else 3), gf)

    def g_near(h):
        g_block(h, 1)
        g_block(h, 3)
        for t in range(4):
            if t in PLUS:
                g_direct(h, 3, t, "gL", at_y(3), gl)
            else:
                g_direct(h, 1, t, "gR", at_y(1), gr)

    def g_relay(h, ts):
        for t in ts:
            arrived(("gF", h, t), gf.at[h, t])
            dy = 1 if t in PLUS else 3
            gps[h, dy, t] = (gpf[h, dy, t] + gf[h, t].astype(F32)).astype(BF)
            if t in PLUS:
                send(("gR", h, t), gps.at[h, dy, t], gr.at[h, t], at_y(1))
            else:
                send(("gL", h, t), gps.at[h, dy, t], gl.at[h, t], at_y(3))

    def g_sum(h, t):
        arrived(("gR", h, t), gr.at[h, t])
        arrived(("gL", h, t), gl.at[h, t])
        return gpf[h, 0, t] + gr[h, t].astype(F32) + gl[h, t].astype(F32)

    def h_block(f):
        group = (vb + f) % 4
        rows = pairs[pl.ds(group * 4, 4), other_c].reshape(448, 512)
        hsib[f] = dot(rows, tb[...], 1, 1).astype(BF).reshape(4, 112, 512)
        send(("hS", f), hsib.at[f], hsibr.at[f], at_x(0, True))
        rows = pairs[pl.ds(group * 4, 4), c].reshape(448, 512)
        hof[f] = dot(rows, tb[...], 1, 1).reshape(4, 112, 512)

    def h_start(f):
        arrived(("hS", f), hsibr.at[f])
        hof[f] += hsibr[f].astype(F32)
        hxs[f, 2] = hof[f, (x + 2) % 4].astype(BF)
        send(("hF", f), hxs.at[f, 2], hf.at[f], at_x(1 if f in PLUS else 3))
        if f in PLUS:
            hxs[f, 3] = hof[f, (x + 3) % 4].astype(BF)
            send(("hL", f), hxs.at[f, 3], hl.at[f], at_x(3))
        else:
            hxs[f, 1] = hof[f, (x + 1) % 4].astype(BF)
            send(("hR", f), hxs.at[f, 1], hr.at[f], at_x(1))

    def h_relay(f):
        arrived(("hF", f), hf.at[f])
        dx = 1 if f in PLUS else 3
        hxs[f, dx] = (hof[f, (x + dx) % 4] + hf[f].astype(F32)).astype(BF)
        if f in PLUS:
            send(("hR", f), hxs.at[f, dx], hr.at[f], at_x(1))
        else:
            send(("hL", f), hxs.at[f, dx], hl.at[f], at_x(3))

    def h_sum(f):
        arrived(("hR", f), hr.at[f])
        arrived(("hL", f), hl.at[f])
        return hof[f, x] + hr[f].astype(F32) + hl[f].astype(F32)

    def h_finish(f):
        hxs[f, 0] = h_sum(f).astype(BF)
        send(("hz", f), hxs.at[f, 0], hz.at[f], at_vb(f))

    def z_out(t):
        gps[1, 0, t] = g_sum(1, t).astype(BF)
        send(("z2", t), gps.at[1, 0, t], zr2.at[t], up2_dev)

    def z_pass(t):
        arrived(("z2", t), zr2.at[t])
        send(("z3", t), zr2.at[t], zs2.at[t], up2_dev)

    g_far(1)
    h_block(2)
    g_near(1)
    h_block(1)
    h_block(3)
    h_start(2)
    h_start(1)
    g_relay(1, (0, 1, 2, 3))
    h_start(3)
    g_far(0)
    h_block(0)
    g_block(1, 0)
    h_relay(2)
    h_relay(1)
    g_near(0)
    z_out(0)
    z_out(1)
    h_relay(3)
    z_out(2)
    z_out(3)
    h_finish(2)
    h_finish(1)
    g_block(0, 0)
    h_start(0)
    h_finish(3)
    z_pass(0)
    z_pass(1)
    g_relay(0, (0, 1, 2, 3))
    h_relay(0)
    z_pass(2)
    z_pass(3)
    total = h_sum(0)
    for f in (1, 3, 2):
        arrived(("hz", f), hz.at[f])
        total = total + hz[f].astype(F32)
    go_ref[...] = total
    for t in range(4):
        part = g_sum(0, t)
        arrived(("z3", t), zs2.at[t])
        gp_ref[t] = part + zs2[t].astype(F32)
    for copy in started:
        copy.wait_send()


def per_device(occ_slab, pair_slab, occ_energy, pair_energy, vir_energy):
    vmem = pl.BlockSpec(memory_space=pltpu.VMEM)
    smem = pl.BlockSpec(memory_space=pltpu.SMEM)
    chunk = (112, 512)
    gamma_occ, gamma_pair = pl.pallas_call(
        kernel,
        out_shape=(jax.ShapeDtypeStruct(chunk, F32), jax.ShapeDtypeStruct((4,) + chunk, F32)),
        in_specs=[vmem, vmem, smem, smem, vmem],
        out_specs=(vmem, vmem),
        scratch_shapes=[
            pltpu.VMEM((8, 56, 512), BF),
            pltpu.VMEM((16, 2) + chunk, BF),
            pltpu.VMEM((4,) + chunk, BF),
            pltpu.VMEM((32,) + chunk, BF),
            pltpu.VMEM((256, 128), F32),
            pltpu.VMEM((512, 512), F32),
            pltpu.VMEM((512, 512), BF),
            pltpu.VMEM((2, 4, 4) + chunk, F32),
            pltpu.VMEM((2, 4, 4) + chunk, BF),
            pltpu.VMEM((2, 4) + chunk, BF),
            pltpu.VMEM((2, 4) + chunk, BF),
            pltpu.VMEM((2, 4) + chunk, BF),
            pltpu.VMEM((4,) + chunk, BF),
            pltpu.VMEM((4,) + chunk, BF),
            pltpu.VMEM((4, 4) + chunk, F32),
            pltpu.VMEM((4, 4) + chunk, BF),
            pltpu.VMEM((4, 4) + chunk, BF),
            pltpu.VMEM((4, 4) + chunk, BF),
            pltpu.VMEM((4,) + chunk, BF),
            pltpu.VMEM((4,) + chunk, BF),
            pltpu.VMEM((4,) + chunk, BF),
            pltpu.VMEM((4,) + chunk, BF),
            pltpu.SemaphoreType.DMA((N_SEMS,)),
            pltpu.SemaphoreType.DMA((N_SEMS,)),
        ],
        compiler_params=pltpu.CompilerParams(
            collective_id=0, has_side_effects=True, vmem_limit_bytes=60 * 1024 * 1024
        ),
        cost_estimate=pl.CostEstimate(flops=5_600_000_000, bytes_accessed=2_000_000, transcendentals=0),
    )(
        occ_slab.reshape(chunk),
        jnp.swapaxes(pair_slab, 0, 1),
        occ_energy,
        pair_energy,
        vir_energy.reshape(1, -1),
    )
    return gamma_occ.reshape(112, 2, 256), gamma_pair.reshape(448, 1, 512)


def solution(mesh):
    placed = (P(("vb", "oj"), None, "va"), P(("va", "oj"), None, "vb"), P(), P("oj"), P())
    return jax.shard_map(
        per_device,
        mesh=mesh,
        in_specs=placed,
        out_specs=(P(("vb", "oj"), None, "va"), P("va", "oj", "vb")),
        check_vma=False,
    )
```

```python
import jax
import jax.numpy as jnp
from jax import lax
from jax.experimental import pallas as pl
from jax.experimental.pallas import tpu as pltpu
from jax.sharding import PartitionSpec as P

MESH = pl.DeviceIdType.MESH
BF = jnp.bfloat16
F32 = jnp.float32
ORDER = (0, 1, 3, 2)
PAIR_DIRECT = ((1, 2),)
OCC_DIRECT = (3,)
PLUS = (0, 3)


def dot(a, b, ca, cb):
    return lax.dot_general(a, b, (((ca,), (cb,)), ((), ())), preferred_element_type=F32)


class Sems:
    def __init__(self, ref, count):
        self.ref, self.count, self.names = ref, count, {}

    def index(self, name):
        at = self.names.setdefault(name, len(self.names))
        assert at < self.count
        return at

    def __getitem__(self, name):
        return self.ref.at[self.index(name)]


N_SEMS = 160


def kernel(
    occ_raw, pair_raw, eo_ref, ep_ref, vir_ref,
    go_ref, gp_ref,
    occ_wide, pair_wide, occ_ref, pair_ref, stage, pairs, occs, ecol, tacc, tb,
    gpf, gps, gr, gl, gf, zs2,
    hof, hsib, hsibr, hxs, hr, hl, hf, hz,
    send_sem, recv_sem,
):
    va, vb, oj = lax.axis_index("va"), lax.axis_index("vb"), lax.axis_index("oj")
    zh, y = va // 4, va % 4
    x, c = oj // 2, oj % 2
    other_c = 1 - c
    ssem, rsem = Sems(send_sem, N_SEMS), Sems(recv_sem, N_SEMS)
    started = {}

    def at_x(dx, dc=False):
        return {"oj": ((x + dx) % 4) * 2 + (other_c if dc else c)}

    def at_y(dy):
        return {"va": zh * 4 + (y + dy) % 4}

    def at_vb(dz):
        return {"vb": (vb + dz) % 4}

    across = {"va": (1 - zh) * 4 + y}

    def send(name, src, dst, dev, when=None, recv_name=None):
        copy = pltpu.make_async_remote_copy(
            src_ref=src, dst_ref=dst, send_sem=ssem[name],
            recv_sem=rsem[name] if recv_name is None else recv_name,
            device_id=dev, device_id_type=MESH,
        )
        started[name] = (copy, when)
        if when is None:
            copy.start()
        else:
            pl.when(when)(copy.start)

    def sent(name):
        copy, when = started.pop(name)
        if when is None:
            copy.wait_send()
        else:
            pl.when(when)(copy.wait_send)

    def arrived(name, dst):
        pltpu.make_async_remote_copy(
            src_ref=dst, dst_ref=dst, send_sem=ssem[name], recv_sem=rsem[name],
            device_id=at_x(0, True), device_id_type=MESH,
        ).wait_recv()

    barrier = pltpu.get_barrier_semaphore()
    partners = [at_x(dx, dc) for dx in range(4) for dc in (False, True) if dx or dc]
    partners += [at_vb(1), at_vb(2), at_vb(3), at_y(1), at_y(2), at_y(3), across]
    for dev in partners:
        pl.semaphore_signal(barrier, inc=1, device_id=dev, device_id_type=MESH)
    for q in range(4):
        pair_wide[q] = pair_raw[:, :, q * 128:(q + 1) * 128].astype(F32).reshape(448, 128)
    for j in range(8):
        for q in range(4):
            pair_ref[j, :, q * 128:(q + 1) * 128] = pair_wide[q, pl.ds(j, 56, stride=8), :].astype(BF)
    occ_wide[...] = occ_raw[...].astype(F32)
    occ_ref[...] = jnp.concatenate([occ_wide[:, 0, :], occ_wide[:, 1, :]], axis=1).astype(BF)
    pl.semaphore_wait(barrier, len(partners))

    def pblk(h, yy, xx):
        hh = zh if h == 0 else 1 - zh
        return pairs.at[(hh * 4 + yy) * 2 + xx // 2, xx % 2]

    def xs(e):
        return (x + 4 - e) % 4

    def zsrc(f):
        step = {0: 0, 1: jnp.where(vb == 0, 3, 1), 2: 2, 3: jnp.where(vb == 0, 1, 3)}[f]
        return (vb + 4 - step) % 4

    def oblk(f, dx, sib=False):
        return occs.at[zsrc(f) * 8 + ((x + dx) % 4) * 2 + (other_c if sib else c)]

    for dx, dc in ((0, True), (1, False), (1, True), (3, False), (3, True), (2, False), (2, True)):
        dev = at_x(dx, dc)
        send(("s1", dx, dc), pair_ref.at[dev["oj"]], stage.at[dx * 2 + int(dc)], dev)
    own_rows = occs.at[vb * 8 + oj]

    oz_at = {f: rsem.index(("oz", f)) for f in (1, 2, 3)}

    def occ_out(f):
        when = {1: vb != 3, 3: vb != 0, 2: None}[f]
        near, other = oz_at[1], oz_at[3]
        slot = {1: near, 2: oz_at[2], 3: jnp.where(vb == 1, near, other)}[f]
        send(("oz", f), occ_ref, own_rows, at_vb(f), when, recv_sem.at[slot])

    occ_out(1)
    occ_out(3)
    own_rows[...] = occ_ref[...]
    stage[0] = pair_ref[oj]

    def occ_spread(f):
        blk = oblk(f, 0)
        send(("oR", f), blk, blk, at_x(1))
        send(("oL", f), blk, blk, at_x(3))
        if f in OCC_DIRECT:
            send(("oF", f), blk, blk, at_x(2))
        send(("oS", 0, f), blk, blk, at_x(0, True))

    def pair_merge(e):
        if e == 0:
            arrived(("s1", 0, True), stage.at[1])
        else:
            for dc in (False, True):
                arrived(("s1", e, dc), stage.at[e * 2 + int(dc)])
        low = stage[e * 2 + c].astype(F32)
        high = stage[e * 2 + other_c].astype(F32)
        blk = pblk(0, y, xs(e))
        blk[...] = jnp.concatenate([low, high], axis=0).astype(BF)
        pair_spread(0, e)

    def pair_spread(h, e):
        blk = pblk(h, y, xs(e))
        send(("yR", h, e), blk, blk, at_y(1))
        send(("yL", h, e), blk, blk, at_y(3))
        if (h, e) in PAIR_DIRECT:
            send(("yF", h, e), blk, blk, at_y(2))

    def z_out1(e):
        blk = pblk(0, y, xs(e))
        send(("zf", e), blk, blk, across)

    def y_forward(h, e):
        right = pblk(h, (y + 3) % 4, xs(e))
        left = pblk(h, (y + 1) % 4, xs(e))
        onward = (h, e) not in PAIR_DIRECT
        if e in PLUS:
            arrived(("yR", h, e), right)
            if onward:
                send(("yF", h, e), right, right, at_y(1))
            arrived(("yL", h, e), left)
        else:
            arrived(("yL", h, e), left)
            if onward:
                send(("yF", h, e), left, left, at_y(3))
            arrived(("yR", h, e), right)

    def occ_forward(f):
        right, left = oblk(f, 3), oblk(f, 1)
        arrived(("oR", f), right)
        if f in PLUS and f not in OCC_DIRECT:
            send(("oF", f), right, right, at_x(1))
        send(("oS", 1, f), right, right, at_x(0, True))
        arrived(("oL", f), left)
        if f not in PLUS and f not in OCC_DIRECT:
            send(("oF", f), left, left, at_x(3))
        send(("oS", 2, f), left, left, at_x(0, True))

    va_row = vir_ref[:, pl.ds(pl.multiple_of(va * 256, 256), 256)]
    ecol[...] = jnp.broadcast_to(va_row, (128, 256)).T
    tacc[...] = jnp.zeros_like(tacc)

    def occ_in(f):
        blk = oblk(f, 0)
        arrived(("oz", f), blk)
        if f == 2:
            other = recv_sem.at[oz_at[3]]
            send(("ozl",), blk, blk, {"vb": 0}, vb == 1, other)
            send(("ozh",), blk, blk, {"vb": 3}, vb == 2, other)
        occ_spread(f)

    def z_in(e):
        arrived(("zf", e), pblk(1, y, xs(e)))
        pair_spread(1, e)

    def occ_far(f):
        far = oblk(f, 2)
        arrived(("oF", f), far)
        send(("oS", 3, f), far, far, at_x(0, True))

    occ_out(2)
    pair_merge(0)
    z_out1(0)
    occ_spread(0)
    pair_merge(1)
    pair_merge(3)
    y_forward(0, 0)
    pair_merge(2)
    occ_in(2)
    z_out1(1)
    y_forward(0, 1)
    occ_in(1)
    occ_in(3)
    y_forward(0, 3)
    sent(("zf", 0))
    z_out1(3)
    z_in(0)
    y_forward(0, 2)
    occ_forward(0)
    sent(("zf", 1))
    z_out1(2)
    z_in(1)
    y_forward(1, 0)
    occ_forward(2)
    z_in(3)
    occ_forward(1)
    occ_far(0)
    y_forward(1, 1)
    z_in(2)
    occ_forward(3)
    occ_far(2)
    y_forward(1, 3)
    occ_far(1)
    occ_far(3)
    y_forward(1, 2)
    for f in ORDER:
        for m, dx in ((0, 0), (1, 3), (2, 1), (3, 2)):
            arrived(("oS", m, f), oblk(f, dx, True))

    def t_add(h, dy):
        hh = zh if h == 0 else 1 - zh
        group = hh * 4 + (y + dy) % 4
        a = occs[pl.ds(group * 4, 4)].reshape(448, 512)
        b = pairs[pl.ds(group * 2, 2)].reshape(448, 512)
        tacc[...] += dot(a, b, 0, 0)

    t_add(0, 0)
    t_add(0, 1)
    t_add(0, 3)
    t_add(1, 0)
    for e in ORDER:
        arrived(("yF", 0, e), pblk(0, (y + 2) % 4, xs(e)))
    t_add(0, 2)
    t_add(1, 1)
    t_add(1, 3)
    for e in ORDER:
        arrived(("yF", 1, e), pblk(1, (y + 2) % 4, xs(e)))
    t_add(1, 2)

    vb_row = vir_ref[:, pl.ds(pl.multiple_of(vb * 512, 512), 512)]
    va_cols = jnp.concatenate([ecol[...]] * 4, axis=1)
    for i in range(2):
        den = ((eo_ref[i] + ep_ref[0]) - va_cols) - vb_row
        tb[i * 256:(i + 1) * 256] = (tacc[i * 256:(i + 1) * 256] / den).astype(BF)

    def g_block(h, dy):
        hh = zh if h == 0 else 1 - zh
        group = hh * 4 + (y + dy) % 4
        rows = occs[pl.ds(group * 4, 4)].reshape(448, 512)
        gpf[h, dy] = dot(rows, tb[...], 1, 0).reshape(4, 112, 512)

    def g_direct(h, dy, t, name, dev, dst):
        gps[h, dy, t] = gpf[h, dy, t].astype(BF)
        send((name, h, t), gps.at[h, dy, t], dst.at[h, t], dev)

    def g_far(h, ts):
        for t in ts:
            g_direct(h, 2, t, "gF", at_y(1 if t in PLUS else 3), gf)

    def g_near(h, ts):
        for t in ts:
            if t in PLUS:
                g_direct(h, 3, t, "gL", at_y(3), gl)
            else:
                g_direct(h, 1, t, "gR", at_y(1), gr)

    def g_relay(h, ts):
        for t in ts:
            arrived(("gF", h, t), gf.at[h, t])
            dy = 1 if t in PLUS else 3
            gps[h, dy, t] = (gpf[h, dy, t] + gf[h, t].astype(F32)).astype(BF)
            if t in PLUS:
                send(("gR", h, t), gps.at[h, dy, t], gr.at[h, t], at_y(1))
            else:
                send(("gL", h, t), gps.at[h, dy, t], gl.at[h, t], at_y(3))

    def g_sum(h, t):
        arrived(("gR", h, t), gr.at[h, t])
        arrived(("gL", h, t), gl.at[h, t])
        return gpf[h, 0, t] + gr[h, t].astype(F32) + gl[h, t].astype(F32)

    def h_block(f):
        group = (vb + f) % 4
        rows = pairs[pl.ds(group * 4, 4), other_c].reshape(448, 512)
        hsib[f] = dot(rows, tb[...], 1, 1).astype(BF).reshape(4, 112, 512)
        send(("hS", f), hsib.at[f], hsibr.at[f], at_x(0, True))
        rows = pairs[pl.ds(group * 4, 4), c].reshape(448, 512)
        hof[f] = dot(rows, tb[...], 1, 1).reshape(4, 112, 512)

    def h_start(f):
        arrived(("hS", f), hsibr.at[f])
        hof[f] += hsibr[f].astype(F32)
        hxs[f, 2] = hof[f, (x + 2) % 4].astype(BF)
        send(("hF", f), hxs.at[f, 2], hf.at[f], at_x(1 if f in PLUS else 3))
        if f in PLUS:
            hxs[f, 3] = hof[f, (x + 3) % 4].astype(BF)
            send(("hL", f), hxs.at[f, 3], hl.at[f], at_x(3))
        else:
            hxs[f, 1] = hof[f, (x + 1) % 4].astype(BF)
            send(("hR", f), hxs.at[f, 1], hr.at[f], at_x(1))

    def h_relay(f):
        arrived(("hF", f), hf.at[f])
        dx = 1 if f in PLUS else 3
        hxs[f, dx] = (hof[f, (x + dx) % 4] + hf[f].astype(F32)).astype(BF)
        if f in PLUS:
            send(("hR", f), hxs.at[f, dx], hr.at[f], at_x(1))
        else:
            send(("hL", f), hxs.at[f, dx], hl.at[f], at_x(3))

    def h_sum(f):
        arrived(("hR", f), hr.at[f])
        arrived(("hL", f), hl.at[f])
        return hof[f, x] + hr[f].astype(F32) + hl[f].astype(F32)

    def h_finish(f):
        hxs[f, 0] = h_sum(f).astype(BF)
        send(("hz", f), hxs.at[f, 0], hz.at[f], at_vb(f))

    def z_out(t):
        gps[1, 0, t] = g_sum(1, t).astype(BF)
        send(("z2", t), gps.at[1, 0, t], zs2.at[t], across)

    g_block(1, 2)
    g_far(1, (0,))
    g_far(1, (1,))
    g_block(1, 1)
    g_block(1, 3)
    g_near(1, (0,))
    g_near(1, (1,))
    h_block(2)
    g_far(1, (3,))
    g_far(1, (2,))
    g_relay(1, (0,))
    g_relay(1, (1,))
    h_block(1)
    h_block(3)
    g_near(1, (3,))
    g_near(1, (2,))
    h_start(2)
    g_block(1, 0)
    h_start(1)
    g_relay(1, (3,))
    g_relay(1, (2,))
    z_out(0)
    z_out(1)
    g_block(0, 2)
    h_start(3)
    h_relay(2)
    g_far(0, (0,))
    g_far(0, (1,))
    h_block(0)
    g_block(0, 1)
    g_block(0, 3)
    g_near(0, (0,))
    g_near(0, (1,))
    h_finish(2)
    h_relay(1)
    z_out(3)
    z_out(2)
    g_far(0, (3,))
    g_far(0, (2,))
    g_relay(0, (0,))
    g_relay(0, (1,))
    h_relay(3)
    h_finish(1)
    g_near(0, (3,))
    g_near(0, (2,))
    h_finish(3)
    g_block(0, 0)
    h_start(0)
    g_relay(0, (3,))
    g_relay(0, (2,))
    h_relay(0)
    total = h_sum(0)
    for f in (1, 3, 2):
        arrived(("hz", f), hz.at[f])
        total = total + hz[f].astype(F32)
    for i in range(2):
        for half in range(2):
            at = i * 256 + half * 128
            go_ref[pl.ds(half * 2 + i, 112, stride=4), :] = total[:, at:at + 128]
    for t in ORDER:
        part = g_sum(0, t)
        arrived(("z2", t), zs2.at[t])
        part = part + zs2[t].astype(F32)
        for q in range(4):
            gp_ref[pl.ds(t * 448 + q, 112, stride=4), :] = part[:, q * 128:(q + 1) * 128]
    for name in list(started):
        sent(name)


def hand_over(go_in, gp_in, go_out, gp_out):
    go_out[...] = go_in[...]
    gp_out[...] = gp_in[...]


def per_device(occ_slab, pair_slab, occ_energy, pair_energy, vir_energy):
    vmem = pl.BlockSpec(memory_space=pltpu.VMEM)
    smem = pl.BlockSpec(memory_space=pltpu.SMEM)
    chunk = (112, 512)
    gamma_occ, gamma_pair = pl.pallas_call(
        kernel,
        out_shape=(jax.ShapeDtypeStruct((448, 128), F32), jax.ShapeDtypeStruct((1792, 128), F32)),
        in_specs=[vmem, vmem, smem, smem, vmem],
        out_specs=(vmem, vmem),
        scratch_shapes=[
            pltpu.VMEM((112, 2, 256), F32),
            pltpu.VMEM((4, 448, 128), F32),
            pltpu.VMEM(chunk, BF),
            pltpu.VMEM((8, 56, 512), BF),
            pltpu.VMEM((8, 56, 512), BF),
            pltpu.VMEM((16, 2) + chunk, BF),
            pltpu.VMEM((32,) + chunk, BF),
            pltpu.VMEM((256, 128), F32),
            pltpu.VMEM((512, 512), F32),
            pltpu.VMEM((512, 512), BF),
            pltpu.VMEM((2, 4, 4) + chunk, F32),
            pltpu.VMEM((2, 4, 4) + chunk, BF),
            pltpu.VMEM((2, 4) + chunk, BF),
            pltpu.VMEM((2, 4) + chunk, BF),
            pltpu.VMEM((2, 4) + chunk, BF),
            pltpu.VMEM((4,) + chunk, BF),
            pltpu.VMEM((4, 4) + chunk, F32),
            pltpu.VMEM((4, 4) + chunk, BF),
            pltpu.VMEM((4, 4) + chunk, BF),
            pltpu.VMEM((4, 4) + chunk, BF),
            pltpu.VMEM((4,) + chunk, BF),
            pltpu.VMEM((4,) + chunk, BF),
            pltpu.VMEM((4,) + chunk, BF),
            pltpu.VMEM((4,) + chunk, BF),
            pltpu.SemaphoreType.DMA((N_SEMS,)),
            pltpu.SemaphoreType.DMA((N_SEMS,)),
        ],
        compiler_params=pltpu.CompilerParams(
            collective_id=0, has_side_effects=True, vmem_limit_bytes=60 * 1024 * 1024
        ),
        cost_estimate=pl.CostEstimate(flops=5_600_000_000, bytes_accessed=2_000_000, transcendentals=0),
    )(
        occ_slab,
        pair_slab,
        occ_energy,
        pair_energy,
        vir_energy.reshape(1, -1),
    )
    gamma_occ, gamma_pair = pl.pallas_call(
        hand_over,
        grid=(2,),
        out_shape=(jax.ShapeDtypeStruct((448, 128), F32), jax.ShapeDtypeStruct((1792, 128), F32)),
        in_specs=[pl.BlockSpec((224, 128), lambda i: (i, 0)), pl.BlockSpec((896, 128), lambda i: (i, 0))],
        out_specs=(pl.BlockSpec((224, 128), lambda i: (i, 0)), pl.BlockSpec((896, 128), lambda i: (i, 0))),
    )(gamma_occ, gamma_pair)
    halves = jnp.swapaxes(gamma_occ.reshape(112, 2, 2, 128), 1, 2)
    return halves.reshape(112, 2, 256), gamma_pair.reshape(448, 1, 512)


def solution(mesh):
    placed = (P(("vb", "oj"), None, "va"), P(("va", "oj"), None, "vb"), P(), P("oj"), P())
    return jax.shard_map(
        per_device,
        mesh=mesh,
        in_specs=placed,
        out_specs=(P(("vb", "oj"), None, "va"), P("va", "oj", "vb")),
        check_vma=False,
    )
```

```python
import jax
import jax.numpy as jnp
from jax import lax
from jax.experimental import pallas as pl
from jax.experimental.pallas import tpu as pltpu
from jax.sharding import PartitionSpec as P

MESH = pl.DeviceIdType.MESH
BF = jnp.bfloat16
F32 = jnp.float32
ORDER = (0, 1, 3, 2)
PAIR_DIRECT = ()
OCC_DIRECT = ()
PLUS = (0, 3)


def dot(a, b, ca, cb):
    return lax.dot_general(a, b, (((ca,), (cb,)), ((), ())), preferred_element_type=F32)


class Sems:
    def __init__(self, ref, count):
        self.ref, self.count, self.names = ref, count, {}

    def index(self, name):
        at = self.names.setdefault(name, len(self.names))
        assert at < self.count
        return at

    def __getitem__(self, name):
        return self.ref.at[self.index(name)]


N_SEMS = 160


def kernel(
    occ_raw, pair_raw, eo_ref, ep_ref, vir_ref,
    go_ref, gp_ref,
    occ_wide, pair_wide, occ_ref, pair_ref, stage, pairs, occs, ecol, tacc, tb,
    gpf, gps, gr, gl, gf, zs2,
    hof, hsib, hsibr, hxs, hr, hl, hf, hz,
    send_sem, recv_sem,
):
    va, vb, oj = lax.axis_index("va"), lax.axis_index("vb"), lax.axis_index("oj")
    zh, y = va // 4, va % 4
    x, c = oj // 2, oj % 2
    other_c = 1 - c
    ssem, rsem = Sems(send_sem, N_SEMS), Sems(recv_sem, N_SEMS)
    started = {}

    def at_x(dx, dc=False):
        return {"oj": ((x + dx) % 4) * 2 + (other_c if dc else c)}

    def at_y(dy):
        return {"va": zh * 4 + (y + dy) % 4}

    def at_vb(dz):
        return {"vb": (vb + dz) % 4}

    across = {"va": (1 - zh) * 4 + y}

    def send(name, src, dst, dev, when=None, recv_name=None):
        copy = pltpu.make_async_remote_copy(
            src_ref=src, dst_ref=dst, send_sem=ssem[name],
            recv_sem=rsem[name] if recv_name is None else recv_name,
            device_id=dev, device_id_type=MESH,
        )
        started[name] = (copy, when)
        if when is None:
            copy.start()
        else:
            pl.when(when)(copy.start)

    def sent(name):
        copy, when = started.pop(name)
        if when is None:
            copy.wait_send()
        else:
            pl.when(when)(copy.wait_send)

    def arrived(name, dst):
        pltpu.make_async_remote_copy(
            src_ref=dst, dst_ref=dst, send_sem=ssem[name], recv_sem=rsem[name],
            device_id=at_x(0, True), device_id_type=MESH,
        ).wait_recv()

    barrier = pltpu.get_barrier_semaphore()
    partners = [at_x(dx, dc) for dx in range(4) for dc in (False, True) if dx or dc]
    partners += [at_vb(1), at_vb(2), at_vb(3), at_y(1), at_y(2), at_y(3), across]
    for dev in partners:
        pl.semaphore_signal(barrier, inc=1, device_id=dev, device_id_type=MESH)
    for q in range(4):
        pair_wide[q] = pair_raw[:, :, q * 128:(q + 1) * 128].astype(F32).reshape(448, 128)
    for j in range(8):
        for q in range(4):
            pair_ref[j, :, q * 128:(q + 1) * 128] = pair_wide[q, pl.ds(j, 56, stride=8), :].astype(BF)
    pl.semaphore_wait(barrier, len(partners))

    def pblk(h, yy, xx):
        hh = zh if h == 0 else 1 - zh
        return pairs.at[(hh * 4 + yy) * 2 + xx // 2, xx % 2]

    def xs(e):
        return (x + 4 - e) % 4

    def zsrc(f):
        step = {0: 0, 1: jnp.where(vb == 0, 3, 1), 2: 2, 3: jnp.where(vb == 0, 1, 3)}[f]
        return (vb + 4 - step) % 4

    def oblk(f, dx, sib=False):
        return occs.at[zsrc(f) * 8 + ((x + dx) % 4) * 2 + (other_c if sib else c)]

    def pair_out(dx):
        for dc in (False, True):
            if dx or dc:
                dev = at_x(dx, dc)
                send(("s1", dx, dc), pair_ref.at[dev["oj"]], stage.at[dx * 2 + int(dc)], dev)

    for dx in (0, 1, 3):
        pair_out(dx)
    occ_wide[...] = occ_raw[...].astype(F32)
    occ_ref[...] = jnp.concatenate([occ_wide[:, 0, :], occ_wide[:, 1, :]], axis=1).astype(BF)
    own_rows = occs.at[vb * 8 + oj]

    oz_at = {f: rsem.index(("oz", f)) for f in (1, 2, 3)}

    def occ_out(f):
        when = {1: vb != 3, 3: vb != 0, 2: None}[f]
        near, other = oz_at[1], oz_at[3]
        slot = {1: near, 2: oz_at[2], 3: jnp.where(vb == 1, near, other)}[f]
        send(("oz", f), occ_ref, own_rows, at_vb(f), when, recv_sem.at[slot])

    occ_out(1)
    occ_out(3)
    own_rows[...] = occ_ref[...]
    stage[0] = pair_ref[oj]

    def occ_spread(f):
        blk = oblk(f, 0)
        send(("oR", f), blk, blk, at_x(1))
        send(("oL", f), blk, blk, at_x(3))
        if f in OCC_DIRECT:
            send(("oF", f), blk, blk, at_x(2))
        send(("oS", 0, f), blk, blk, at_x(0, True))

    def pair_merge(e):
        if e == 0:
            arrived(("s1", 0, True), stage.at[1])
        else:
            for dc in (False, True):
                arrived(("s1", e, dc), stage.at[e * 2 + int(dc)])
        low = stage[e * 2 + c].astype(F32)
        high = stage[e * 2 + other_c].astype(F32)
        blk = pblk(0, y, xs(e))
        blk[...] = jnp.concatenate([low, high], axis=0).astype(BF)
        pair_spread(0, e)

    def pair_spread(h, e):
        blk = pblk(h, y, xs(e))
        send(("yR", h, e), blk, blk, at_y(1))
        send(("yL", h, e), blk, blk, at_y(3))
        if (h, e) in PAIR_DIRECT:
            send(("yF", h, e), blk, blk, at_y(2))

    def z_out1(e):
        blk = pblk(0, y, xs(e))
        send(("zf", e), blk, blk, across)

    def y_forward(h, e):
        right = pblk(h, (y + 3) % 4, xs(e))
        left = pblk(h, (y + 1) % 4, xs(e))
        onward = (h, e) not in PAIR_DIRECT
        if e in PLUS:
            arrived(("yR", h, e), right)
            if onward:
                send(("yF", h, e), right, right, at_y(1))
            arrived(("yL", h, e), left)
        else:
            arrived(("yL", h, e), left)
            if onward:
                send(("yF", h, e), left, left, at_y(3))
            arrived(("yR", h, e), right)

    def occ_forward(f):
        right, left = oblk(f, 3), oblk(f, 1)
        arrived(("oR", f), right)
        if f in PLUS and f not in OCC_DIRECT:
            send(("oF", f), right, right, at_x(1))
        send(("oS", 1, f), right, right, at_x(0, True))
        arrived(("oL", f), left)
        if f not in PLUS and f not in OCC_DIRECT:
            send(("oF", f), left, left, at_x(3))
        send(("oS", 2, f), left, left, at_x(0, True))

    va_row = vir_ref[:, pl.ds(pl.multiple_of(va * 256, 256), 256)]
    ecol[...] = jnp.broadcast_to(va_row, (128, 256)).T
    tacc[...] = jnp.zeros_like(tacc)

    def occ_in(f):
        blk = oblk(f, 0)
        arrived(("oz", f), blk)
        if f == 2:
            other = recv_sem.at[oz_at[3]]
            send(("ozl",), blk, blk, {"vb": 0}, vb == 1, other)
            send(("ozh",), blk, blk, {"vb": 3}, vb == 2, other)
        occ_spread(f)

    def z_in(e):
        arrived(("zf", e), pblk(1, y, xs(e)))
        pair_spread(1, e)

    def occ_far(f):
        far = oblk(f, 2)
        arrived(("oF", f), far)
        send(("oS", 3, f), far, far, at_x(0, True))

    def occ_all(f):
        for m, dx in ((0, 0), (1, 3), (2, 1), (3, 2)):
            arrived(("oS", m, f), oblk(f, dx, True))

    def pair_far(h, e):
        arrived(("yF", h, e), pblk(h, (y + 2) % 4, xs(e)))

    def t_add(h, dy):
        hh = zh if h == 0 else 1 - zh
        group = hh * 4 + (y + dy) % 4
        a = occs[pl.ds(group * 4, 4)].reshape(448, 512)
        b = pairs[pl.ds(group * 2, 2)].reshape(448, 512)
        tacc[...] += dot(a, b, 0, 0)

    pair_out(2)
    occ_out(2)
    pair_merge(0)
    z_out1(0)
    occ_spread(0)
    pair_merge(1)
    pair_merge(3)
    y_forward(0, 0)
    pair_merge(2)
    occ_in(2)
    z_out1(1)
    y_forward(0, 1)
    occ_in(1)
    occ_in(3)
    y_forward(0, 3)
    sent(("zf", 0))
    z_out1(3)
    z_in(0)
    y_forward(0, 2)
    occ_forward(0)
    sent(("zf", 1))
    z_out1(2)
    occ_forward(2)
    z_in(1)
    occ_forward(1)
    y_forward(1, 0)
    occ_far(0)
    occ_forward(3)
    z_in(3)
    occ_far(2)
    occ_far(1)
    y_forward(1, 1)
    occ_far(3)
    pair_far(0, 0)
    pair_far(0, 1)
    pair_far(0, 3)
    pair_far(0, 2)
    z_in(2)
    occ_all(0)
    occ_all(1)
    occ_all(3)
    occ_all(2)
    t_add(0, 0)
    t_add(0, 1)
    t_add(0, 3)
    t_add(0, 2)
    t_add(1, 0)
    y_forward(1, 3)
    y_forward(1, 2)
    t_add(1, 1)
    t_add(1, 3)
    pair_far(1, 0)
    pair_far(1, 1)
    pair_far(1, 3)
    pair_far(1, 2)
    t_add(1, 2)
    vb_row = vir_ref[:, pl.ds(pl.multiple_of(vb * 512, 512), 512)]
    va_cols = jnp.concatenate([ecol[...]] * 4, axis=1)
    for i in range(2):
        den = ((eo_ref[i] + ep_ref[0]) - va_cols) - vb_row
        tb[i * 256:(i + 1) * 256] = (tacc[i * 256:(i + 1) * 256] / den).astype(BF)

    def g_block(h, dy):
        hh = zh if h == 0 else 1 - zh
        group = hh * 4 + (y + dy) % 4
        rows = occs[pl.ds(group * 4, 4)].reshape(448, 512)
        gpf[h, dy] = dot(rows, tb[...], 1, 0).reshape(4, 112, 512)

    def g_direct(h, dy, t, name, dev, dst):
        gps[h, dy, t] = gpf[h, dy, t].astype(BF)
        send((name, h, t), gps.at[h, dy, t], dst.at[h, t], dev)

    def g_far(h, ts):
        for t in ts:
            g_direct(h, 2, t, "gF", at_y(1 if t in PLUS else 3), gf)

    def g_near(h, ts):
        for t in ts:
            if t in PLUS:
                g_direct(h, 3, t, "gL", at_y(3), gl)
            else:
                g_direct(h, 1, t, "gR", at_y(1), gr)

    def g_relay(h, ts):
        for t in ts:
            arrived(("gF", h, t), gf.at[h, t])
            dy = 1 if t in PLUS else 3
            gps[h, dy, t] = (gpf[h, dy, t] + gf[h, t].astype(F32)).astype(BF)
            if t in PLUS:
                send(("gR", h, t), gps.at[h, dy, t], gr.at[h, t], at_y(1))
            else:
                send(("gL", h, t), gps.at[h, dy, t], gl.at[h, t], at_y(3))

    def g_sum(h, t):
        arrived(("gR", h, t), gr.at[h, t])
        arrived(("gL", h, t), gl.at[h, t])
        return gpf[h, 0, t] + gr[h, t].astype(F32) + gl[h, t].astype(F32)

    def h_block(f):
        group = (vb + f) % 4
        rows = pairs[pl.ds(group * 4, 4), other_c].reshape(448, 512)
        hsib[f] = dot(rows, tb[...], 1, 1).astype(BF).reshape(4, 112, 512)
        send(("hS", f), hsib.at[f], hsibr.at[f], at_x(0, True))
        rows = pairs[pl.ds(group * 4, 4), c].reshape(448, 512)
        hof[f] = dot(rows, tb[...], 1, 1).reshape(4, 112, 512)

    def h_start(f):
        arrived(("hS", f), hsibr.at[f])
        hof[f] += hsibr[f].astype(F32)
        hxs[f, 2] = hof[f, (x + 2) % 4].astype(BF)
        send(("hF", f), hxs.at[f, 2], hf.at[f], at_x(1 if f in PLUS else 3))
        if f in PLUS:
            hxs[f, 3] = hof[f, (x + 3) % 4].astype(BF)
            send(("hL", f), hxs.at[f, 3], hl.at[f], at_x(3))
        else:
            hxs[f, 1] = hof[f, (x + 1) % 4].astype(BF)
            send(("hR", f), hxs.at[f, 1], hr.at[f], at_x(1))

    def h_relay(f):
        arrived(("hF", f), hf.at[f])
        dx = 1 if f in PLUS else 3
        hxs[f, dx] = (hof[f, (x + dx) % 4] + hf[f].astype(F32)).astype(BF)
        if f in PLUS:
            send(("hR", f), hxs.at[f, dx], hr.at[f], at_x(1))
        else:
            send(("hL", f), hxs.at[f, dx], hl.at[f], at_x(3))

    def h_sum(f):
        arrived(("hR", f), hr.at[f])
        arrived(("hL", f), hl.at[f])
        return hof[f, x] + hr[f].astype(F32) + hl[f].astype(F32)

    def h_finish(f):
        hxs[f, 0] = h_sum(f).astype(BF)
        send(("hz", f), hxs.at[f, 0], hz.at[f], at_vb(f))

    def z_out(t):
        gps[1, 0, t] = g_sum(1, t).astype(BF)
        send(("z2", t), gps.at[1, 0, t], zs2.at[t], across)

    g_block(1, 2)
    g_far(1, (0,))
    g_far(1, (1,))
    g_block(1, 1)
    g_block(1, 3)
    g_near(1, (0,))
    g_near(1, (1,))
    h_block(2)
    g_far(1, (3,))
    g_far(1, (2,))
    g_relay(1, (0,))
    g_relay(1, (1,))
    h_block(1)
    h_block(3)
    g_near(1, (3,))
    g_near(1, (2,))
    h_start(2)
    g_block(1, 0)
    h_start(1)
    g_relay(1, (3,))
    g_relay(1, (2,))
    z_out(0)
    z_out(1)
    g_block(0, 2)
    h_start(3)
    h_relay(2)
    g_far(0, (0,))
    g_far(0, (1,))
    h_block(0)
    g_block(0, 1)
    g_block(0, 3)
    g_near(0, (0,))
    g_near(0, (1,))
    h_finish(2)
    h_relay(1)
    z_out(3)
    z_out(2)
    g_far(0, (3,))
    g_far(0, (2,))
    g_relay(0, (0,))
    g_relay(0, (1,))
    h_relay(3)
    h_finish(1)
    g_near(0, (3,))
    g_near(0, (2,))
    h_finish(3)
    g_block(0, 0)
    h_start(0)
    g_relay(0, (3,))
    g_relay(0, (2,))
    h_relay(0)
    total = h_sum(0)
    for f in (1, 3, 2):
        arrived(("hz", f), hz.at[f])
        total = total + hz[f].astype(F32)
    for i in range(2):
        for half in range(2):
            at = i * 256 + half * 128
            go_ref[pl.ds(half * 2 + i, 112, stride=4), :] = total[:, at:at + 128]
    for t in ORDER:
        part = g_sum(0, t)
        arrived(("z2", t), zs2.at[t])
        part = part + zs2[t].astype(F32)
        for q in range(4):
            gp_ref[pl.ds(t * 448 + q, 112, stride=4), :] = part[:, q * 128:(q + 1) * 128]
    for name in list(started):
        sent(name)


def hand_over(go_in, gp_in, go_out, gp_out):
    go_out[...] = go_in[...]
    gp_out[...] = gp_in[...]


def per_device(occ_slab, pair_slab, occ_energy, pair_energy, vir_energy):
    vmem = pl.BlockSpec(memory_space=pltpu.VMEM)
    smem = pl.BlockSpec(memory_space=pltpu.SMEM)
    chunk = (112, 512)
    gamma_occ, gamma_pair = pl.pallas_call(
        kernel,
        out_shape=(jax.ShapeDtypeStruct((448, 128), F32), jax.ShapeDtypeStruct((1792, 128), F32)),
        in_specs=[vmem, vmem, smem, smem, vmem],
        out_specs=(vmem, vmem),
        scratch_shapes=[
            pltpu.VMEM((112, 2, 256), F32),
            pltpu.VMEM((4, 448, 128), F32),
            pltpu.VMEM(chunk, BF),
            pltpu.VMEM((8, 56, 512), BF),
            pltpu.VMEM((8, 56, 512), BF),
            pltpu.VMEM((16, 2) + chunk, BF),
            pltpu.VMEM((32,) + chunk, BF),
            pltpu.VMEM((256, 128), F32),
            pltpu.VMEM((512, 512), F32),
            pltpu.VMEM((512, 512), BF),
            pltpu.VMEM((2, 4, 4) + chunk, F32),
            pltpu.VMEM((2, 4, 4) + chunk, BF),
            pltpu.VMEM((2, 4) + chunk, BF),
            pltpu.VMEM((2, 4) + chunk, BF),
            pltpu.VMEM((2, 4) + chunk, BF),
            pltpu.VMEM((4,) + chunk, BF),
            pltpu.VMEM((4, 4) + chunk, F32),
            pltpu.VMEM((4, 4) + chunk, BF),
            pltpu.VMEM((4, 4) + chunk, BF),
            pltpu.VMEM((4, 4) + chunk, BF),
            pltpu.VMEM((4,) + chunk, BF),
            pltpu.VMEM((4,) + chunk, BF),
            pltpu.VMEM((4,) + chunk, BF),
            pltpu.VMEM((4,) + chunk, BF),
            pltpu.SemaphoreType.DMA((N_SEMS,)),
            pltpu.SemaphoreType.DMA((N_SEMS,)),
        ],
        compiler_params=pltpu.CompilerParams(
            collective_id=0, has_side_effects=True, vmem_limit_bytes=60 * 1024 * 1024
        ),
        cost_estimate=pl.CostEstimate(flops=5_600_000_000, bytes_accessed=2_000_000, transcendentals=0),
    )(
        occ_slab,
        pair_slab,
        occ_energy,
        pair_energy,
        vir_energy.reshape(1, -1),
    )
    gamma_occ, gamma_pair = pl.pallas_call(
        hand_over,
        grid=(2,),
        out_shape=(jax.ShapeDtypeStruct((448, 128), F32), jax.ShapeDtypeStruct((1792, 128), F32)),
        in_specs=[pl.BlockSpec((224, 128), lambda i: (i, 0)), pl.BlockSpec((896, 128), lambda i: (i, 0))],
        out_specs=(pl.BlockSpec((224, 128), lambda i: (i, 0)), pl.BlockSpec((896, 128), lambda i: (i, 0))),
    )(gamma_occ, gamma_pair)
    halves = jnp.swapaxes(gamma_occ.reshape(112, 2, 2, 128), 1, 2)
    return halves.reshape(112, 2, 256), gamma_pair.reshape(448, 1, 512)


def solution(mesh):
    placed = (P(("vb", "oj"), None, "va"), P(("va", "oj"), None, "vb"), P(), P("oj"), P())
    return jax.shard_map(
        per_device,
        mesh=mesh,
        in_specs=placed,
        out_specs=(P(("vb", "oj"), None, "va"), P("va", "oj", "vb")),
        check_vma=False,
    )
```

```python
import jax
import jax.numpy as jnp
from jax import lax
from jax.experimental import pallas as pl
from jax.experimental.pallas import tpu as pltpu
from jax.sharding import PartitionSpec as P

MESH = pl.DeviceIdType.MESH
BF = jnp.bfloat16
F32 = jnp.float32
ORDER = (0, 1, 3, 2)
PAIR_DIRECT = ()
OCC_DIRECT = ()
PLUS = (0, 3)


def dot(a, b, ca, cb):
    return lax.dot_general(a, b, (((ca,), (cb,)), ((), ())), preferred_element_type=F32)


class Sems:
    def __init__(self, ref, count):
        self.ref, self.count, self.names = ref, count, {}

    def index(self, name):
        at = self.names.setdefault(name, len(self.names))
        assert at < self.count
        return at

    def __getitem__(self, name):
        return self.ref.at[self.index(name)]


N_SEMS = 160


def kernel(
    occ_raw, pair_raw, eo_ref, ep_ref, vir_ref,
    go_ref, gp_ref,
    occ_wide, pair_wide, occ_ref, pair_ref, stage, pairs, occs, ecol, tacc, tb,
    gpf, gps, gr, gl, gf, zs2,
    hof, hsib, hsibr, hxs, hr, hl, hf, hz,
    send_sem, recv_sem,
):
    va, vb, oj = lax.axis_index("va"), lax.axis_index("vb"), lax.axis_index("oj")
    zh, y = va // 4, va % 4
    x, c = oj // 2, oj % 2
    other_c = 1 - c
    ssem, rsem = Sems(send_sem, N_SEMS), Sems(recv_sem, N_SEMS)
    started = {}

    def at_x(dx, dc=False):
        return {"oj": ((x + dx) % 4) * 2 + (other_c if dc else c)}

    def at_y(dy):
        return {"va": zh * 4 + (y + dy) % 4}

    def at_vb(dz):
        return {"vb": (vb + dz) % 4}

    across = {"va": (1 - zh) * 4 + y}

    def send(name, src, dst, dev, when=None, recv_name=None):
        copy = pltpu.make_async_remote_copy(
            src_ref=src, dst_ref=dst, send_sem=ssem[name],
            recv_sem=rsem[name] if recv_name is None else recv_name,
            device_id=dev, device_id_type=MESH,
        )
        started[name] = (copy, when)
        if when is None:
            copy.start()
        else:
            pl.when(when)(copy.start)

    def sent(name):
        copy, when = started.pop(name)
        if when is None:
            copy.wait_send()
        else:
            pl.when(when)(copy.wait_send)

    def arrived(name, dst):
        pltpu.make_async_remote_copy(
            src_ref=dst, dst_ref=dst, send_sem=ssem[name], recv_sem=rsem[name],
            device_id=at_x(0, True), device_id_type=MESH,
        ).wait_recv()

    barrier = pltpu.get_barrier_semaphore()
    partners = [at_x(dx, dc) for dx in range(4) for dc in (False, True) if dx or dc]
    partners += [at_vb(1), at_vb(2), at_vb(3), at_y(1), at_y(2), at_y(3), across]
    for dev in partners:
        pl.semaphore_signal(barrier, inc=1, device_id=dev, device_id_type=MESH)
    for q in range(4):
        pair_wide[q] = pair_raw[:, :, q * 128:(q + 1) * 128].astype(F32).reshape(448, 128)
    for j in range(8):
        for q in range(4):
            pair_ref[j, :, q * 128:(q + 1) * 128] = pair_wide[q, pl.ds(j, 56, stride=8), :].astype(BF)
    pl.semaphore_wait(barrier, len(partners))

    def pblk(h, yy, xx):
        hh = zh if h == 0 else 1 - zh
        return pairs.at[(hh * 4 + yy) * 2 + xx // 2, xx % 2]

    def xs(e):
        return (x + 4 - e) % 4

    def zsrc(f):
        step = {0: 0, 1: jnp.where(vb == 0, 3, 1), 2: 2, 3: jnp.where(vb == 0, 1, 3)}[f]
        return (vb + 4 - step) % 4

    def oblk(f, dx, sib=False):
        return occs.at[zsrc(f) * 8 + ((x + dx) % 4) * 2 + (other_c if sib else c)]

    def pair_out(dx):
        for dc in (False, True):
            if dx or dc:
                dev = at_x(dx, dc)
                send(("s1", dx, dc), pair_ref.at[dev["oj"]], stage.at[dx * 2 + int(dc)], dev)

    for dx in (0, 1, 3):
        pair_out(dx)
    occ_wide[...] = occ_raw[...].astype(F32)
    occ_ref[...] = jnp.concatenate([occ_wide[:, 0, :], occ_wide[:, 1, :]], axis=1).astype(BF)
    own_rows = occs.at[vb * 8 + oj]

    oz_at = {f: rsem.index(("oz", f)) for f in (1, 2, 3)}

    def occ_out(f):
        when = {1: vb != 3, 3: vb != 0, 2: None}[f]
        near, other = oz_at[1], oz_at[3]
        slot = {1: near, 2: oz_at[2], 3: jnp.where(vb == 1, near, other)}[f]
        send(("oz", f), occ_ref, own_rows, at_vb(f), when, recv_sem.at[slot])

    occ_out(1)
    occ_out(3)
    own_rows[...] = occ_ref[...]
    stage[0] = pair_ref[oj]

    def occ_spread(f):
        blk = oblk(f, 0)
        send(("oR", f), blk, blk, at_x(1))
        send(("oL", f), blk, blk, at_x(3))
        if f in OCC_DIRECT:
            send(("oF", f), blk, blk, at_x(2))
        send(("oS", 0, f), blk, blk, at_x(0, True))

    def pair_merge(e):
        if e == 0:
            arrived(("s1", 0, True), stage.at[1])
        else:
            for dc in (False, True):
                arrived(("s1", e, dc), stage.at[e * 2 + int(dc)])
        low = stage[e * 2 + c].astype(F32)
        high = stage[e * 2 + other_c].astype(F32)
        blk = pblk(0, y, xs(e))
        blk[...] = jnp.concatenate([low, high], axis=0).astype(BF)
        pair_spread(0, e)

    def pair_spread(h, e):
        blk = pblk(h, y, xs(e))
        send(("yR", h, e), blk, blk, at_y(1))
        send(("yL", h, e), blk, blk, at_y(3))
        if (h, e) in PAIR_DIRECT:
            send(("yF", h, e), blk, blk, at_y(2))

    def z_out1(e):
        blk = pblk(0, y, xs(e))
        send(("zf", e), blk, blk, across)

    def y_forward(h, e):
        right = pblk(h, (y + 3) % 4, xs(e))
        left = pblk(h, (y + 1) % 4, xs(e))
        onward = (h, e) not in PAIR_DIRECT
        if e in PLUS:
            arrived(("yR", h, e), right)
            if onward:
                send(("yF", h, e), right, right, at_y(1))
            arrived(("yL", h, e), left)
        else:
            arrived(("yL", h, e), left)
            if onward:
                send(("yF", h, e), left, left, at_y(3))
            arrived(("yR", h, e), right)

    def occ_forward(f):
        right, left = oblk(f, 3), oblk(f, 1)
        arrived(("oR", f), right)
        if f in PLUS and f not in OCC_DIRECT:
            send(("oF", f), right, right, at_x(1))
        send(("oS", 1, f), right, right, at_x(0, True))
        arrived(("oL", f), left)
        if f not in PLUS and f not in OCC_DIRECT:
            send(("oF", f), left, left, at_x(3))
        send(("oS", 2, f), left, left, at_x(0, True))

    va_row = vir_ref[:, pl.ds(pl.multiple_of(va * 256, 256), 256)]
    ecol[...] = jnp.broadcast_to(va_row, (128, 256)).T
    tacc[...] = jnp.zeros_like(tacc)

    def occ_in(f):
        blk = oblk(f, 0)
        arrived(("oz", f), blk)
        if f == 2:
            other = recv_sem.at[oz_at[3]]
            send(("ozl",), blk, blk, {"vb": 0}, vb == 1, other)
            send(("ozh",), blk, blk, {"vb": 3}, vb == 2, other)
        occ_spread(f)

    def z_in(e):
        arrived(("zf", e), pblk(1, y, xs(e)))
        pair_spread(1, e)

    def occ_far(f):
        far = oblk(f, 2)
        arrived(("oF", f), far)
        send(("oS", 3, f), far, far, at_x(0, True))

    def occ_all(f):
        for m, dx in ((0, 0), (1, 3), (2, 1), (3, 2)):
            arrived(("oS", m, f), oblk(f, dx, True))

    def pair_far(h, e):
        arrived(("yF", h, e), pblk(h, (y + 2) % 4, xs(e)))

    def t_add(h, dy):
        hh = zh if h == 0 else 1 - zh
        group = hh * 4 + (y + dy) % 4
        a = occs[pl.ds(group * 4, 4)].reshape(448, 512)
        b = pairs[pl.ds(group * 2, 2)].reshape(448, 512)
        tacc[...] += dot(a, b, 0, 0)

    pair_out(2)
    occ_out(2)
    pair_merge(0)
    z_out1(0)
    occ_spread(0)
    pair_merge(1)
    pair_merge(3)
    y_forward(0, 0)
    pair_merge(2)
    occ_in(2)
    z_out1(1)
    y_forward(0, 1)
    occ_in(1)
    occ_in(3)
    y_forward(0, 3)
    sent(("zf", 0))
    z_out1(3)
    z_in(0)
    y_forward(0, 2)
    occ_forward(0)
    sent(("zf", 1))
    z_out1(2)
    occ_forward(2)
    z_in(1)
    occ_forward(1)
    y_forward(1, 0)
    occ_far(0)
    occ_forward(3)
    z_in(3)
    occ_far(2)
    occ_far(1)
    y_forward(1, 1)
    occ_far(3)
    pair_far(0, 0)
    pair_far(0, 1)
    pair_far(0, 3)
    pair_far(0, 2)
    z_in(2)
    occ_all(0)
    occ_all(1)
    occ_all(3)
    occ_all(2)
    t_add(0, 0)
    t_add(0, 1)
    t_add(0, 3)
    t_add(0, 2)
    t_add(1, 0)
    y_forward(1, 3)
    y_forward(1, 2)
    t_add(1, 1)
    t_add(1, 3)
    pair_far(1, 0)
    pair_far(1, 1)
    pair_far(1, 3)
    pair_far(1, 2)
    t_add(1, 2)
    vb_row = vir_ref[:, pl.ds(pl.multiple_of(vb * 512, 512), 512)]
    va_cols = jnp.concatenate([ecol[...]] * 4, axis=1)
    for i in range(2):
        den = ((eo_ref[i] + ep_ref[0]) - va_cols) - vb_row
        tb[i * 256:(i + 1) * 256] = (tacc[i * 256:(i + 1) * 256] / den).astype(BF)

    def g_block(h, dy):
        hh = zh if h == 0 else 1 - zh
        group = hh * 4 + (y + dy) % 4
        rows = occs[pl.ds(group * 4, 4)].reshape(448, 512)
        gpf[h, dy] = dot(rows, tb[...], 1, 0).reshape(4, 112, 512)

    def g_direct(h, dy, t, name, dev, dst):
        gps[h, dy, t] = gpf[h, dy, t].astype(BF)
        send((name, h, t), gps.at[h, dy, t], dst.at[h, t], dev)

    def g_far(h, ts):
        for t in ts:
            g_direct(h, 2, t, "gF", at_y(1 if t in PLUS else 3), gf)

    def g_near(h, ts):
        for t in ts:
            if t in PLUS:
                g_direct(h, 3, t, "gL", at_y(3), gl)
            else:
                g_direct(h, 1, t, "gR", at_y(1), gr)

    def g_relay(h, ts):
        for t in ts:
            arrived(("gF", h, t), gf.at[h, t])
            dy = 1 if t in PLUS else 3
            gps[h, dy, t] = (gpf[h, dy, t] + gf[h, t].astype(F32)).astype(BF)
            if t in PLUS:
                send(("gR", h, t), gps.at[h, dy, t], gr.at[h, t], at_y(1))
            else:
                send(("gL", h, t), gps.at[h, dy, t], gl.at[h, t], at_y(3))

    def g_sum(h, t):
        arrived(("gR", h, t), gr.at[h, t])
        arrived(("gL", h, t), gl.at[h, t])
        return gpf[h, 0, t] + gr[h, t].astype(F32) + gl[h, t].astype(F32)

    def h_block(f):
        group = (vb + f) % 4
        rows = pairs[pl.ds(group * 4, 4), other_c].reshape(448, 512)
        hsib[f] = dot(rows, tb[...], 1, 1).astype(BF).reshape(4, 112, 512)
        send(("hS", f), hsib.at[f], hsibr.at[f], at_x(0, True))
        rows = pairs[pl.ds(group * 4, 4), c].reshape(448, 512)
        hof[f] = dot(rows, tb[...], 1, 1).reshape(4, 112, 512)

    def h_start(f):
        arrived(("hS", f), hsibr.at[f])
        hof[f] += hsibr[f].astype(F32)
        hxs[f, 2] = hof[f, (x + 2) % 4].astype(BF)
        send(("hF", f), hxs.at[f, 2], hf.at[f], at_x(1 if f in PLUS else 3))
        if f in PLUS:
            hxs[f, 3] = hof[f, (x + 3) % 4].astype(BF)
            send(("hL", f), hxs.at[f, 3], hl.at[f], at_x(3))
        else:
            hxs[f, 1] = hof[f, (x + 1) % 4].astype(BF)
            send(("hR", f), hxs.at[f, 1], hr.at[f], at_x(1))

    def h_relay(f):
        arrived(("hF", f), hf.at[f])
        dx = 1 if f in PLUS else 3
        hxs[f, dx] = (hof[f, (x + dx) % 4] + hf[f].astype(F32)).astype(BF)
        if f in PLUS:
            send(("hR", f), hxs.at[f, dx], hr.at[f], at_x(1))
        else:
            send(("hL", f), hxs.at[f, dx], hl.at[f], at_x(3))

    def h_sum(f):
        arrived(("hR", f), hr.at[f])
        arrived(("hL", f), hl.at[f])
        return hof[f, x] + hr[f].astype(F32) + hl[f].astype(F32)

    def h_finish(f):
        hxs[f, 0] = h_sum(f).astype(BF)
        send(("hz", f), hxs.at[f, 0], hz.at[f], at_vb(f))

    def z_out(t):
        gps[1, 0, t] = g_sum(1, t).astype(BF)
        send(("z2", t), gps.at[1, 0, t], zs2.at[t], across)

    g_block(1, 2)
    g_far(1, (0,))
    g_far(1, (1,))
    g_block(1, 1)
    g_block(1, 3)
    g_near(1, (0,))
    g_near(1, (1,))
    h_block(2)
    g_far(1, (3,))
    g_far(1, (2,))
    g_relay(1, (0,))
    g_relay(1, (1,))
    h_block(1)
    h_block(3)
    g_near(1, (3,))
    g_near(1, (2,))
    h_start(2)
    g_block(1, 0)
    h_start(1)
    g_relay(1, (3,))
    g_relay(1, (2,))
    z_out(0)
    z_out(1)
    g_block(0, 2)
    h_start(3)
    h_relay(2)
    g_far(0, (0,))
    g_far(0, (1,))
    h_block(0)
    g_block(0, 1)
    g_block(0, 3)
    g_near(0, (0,))
    g_near(0, (1,))
    h_finish(2)
    h_relay(1)
    z_out(3)
    z_out(2)
    g_far(0, (3,))
    g_far(0, (2,))
    g_relay(0, (0,))
    g_relay(0, (1,))
    h_relay(3)
    h_finish(1)
    g_near(0, (3,))
    g_near(0, (2,))
    h_finish(3)
    g_block(0, 0)
    h_start(0)
    g_relay(0, (3,))
    g_relay(0, (2,))
    h_relay(0)
    for name in list(started):
        if name[0] not in ("gR", "gL", "z2", "hz", "hR", "hL"):
            sent(name)
    total = h_sum(0)
    for f in (1, 3, 2):
        arrived(("hz", f), hz.at[f])
        total = total + hz[f].astype(F32)
    for i in range(2):
        for half in range(2):
            at = i * 256 + half * 128
            go_ref[pl.ds(half * 2 + i, 112, stride=4), :] = total[:, at:at + 128]
    for t in ORDER:
        part = g_sum(0, t)
        arrived(("z2", t), zs2.at[t])
        part = part + zs2[t].astype(F32)
        for q in range(4):
            gp_ref[pl.ds(t * 448 + q, 112, stride=4), :] = part[:, q * 128:(q + 1) * 128]
    for name in list(started):
        sent(name)


def hand_over(go_in, gp_in, go_out, gp_out):
    go_out[...] = go_in[...]
    gp_out[...] = gp_in[...]


def per_device(occ_slab, pair_slab, occ_energy, pair_energy, vir_energy):
    vmem = pl.BlockSpec(memory_space=pltpu.VMEM)
    smem = pl.BlockSpec(memory_space=pltpu.SMEM)
    chunk = (112, 512)
    gamma_occ, gamma_pair = pl.pallas_call(
        kernel,
        out_shape=(jax.ShapeDtypeStruct((448, 128), F32), jax.ShapeDtypeStruct((1792, 128), F32)),
        in_specs=[vmem, vmem, smem, smem, vmem],
        out_specs=(vmem, vmem),
        scratch_shapes=[
            pltpu.VMEM((112, 2, 256), F32),
            pltpu.VMEM((4, 448, 128), F32),
            pltpu.VMEM(chunk, BF),
            pltpu.VMEM((8, 56, 512), BF),
            pltpu.VMEM((8, 56, 512), BF),
            pltpu.VMEM((16, 2) + chunk, BF),
            pltpu.VMEM((32,) + chunk, BF),
            pltpu.VMEM((256, 128), F32),
            pltpu.VMEM((512, 512), F32),
            pltpu.VMEM((512, 512), BF),
            pltpu.VMEM((2, 4, 4) + chunk, F32),
            pltpu.VMEM((2, 4, 4) + chunk, BF),
            pltpu.VMEM((2, 4) + chunk, BF),
            pltpu.VMEM((2, 4) + chunk, BF),
            pltpu.VMEM((2, 4) + chunk, BF),
            pltpu.VMEM((4,) + chunk, BF),
            pltpu.VMEM((4, 4) + chunk, F32),
            pltpu.VMEM((4, 4) + chunk, BF),
            pltpu.VMEM((4, 4) + chunk, BF),
            pltpu.VMEM((4, 4) + chunk, BF),
            pltpu.VMEM((4,) + chunk, BF),
            pltpu.VMEM((4,) + chunk, BF),
            pltpu.VMEM((4,) + chunk, BF),
            pltpu.VMEM((4,) + chunk, BF),
            pltpu.SemaphoreType.DMA((N_SEMS,)),
            pltpu.SemaphoreType.DMA((N_SEMS,)),
        ],
        compiler_params=pltpu.CompilerParams(
            collective_id=0, has_side_effects=True, vmem_limit_bytes=60 * 1024 * 1024
        ),
        cost_estimate=pl.CostEstimate(flops=5_600_000_000, bytes_accessed=2_000_000, transcendentals=0),
    )(
        occ_slab,
        pair_slab,
        occ_energy,
        pair_energy,
        vir_energy.reshape(1, -1),
    )
    gamma_occ, gamma_pair = pl.pallas_call(
        hand_over,
        out_shape=(jax.ShapeDtypeStruct((448, 128), F32), jax.ShapeDtypeStruct((1792, 128), F32)),
        in_specs=[vmem, vmem],
        out_specs=(vmem, vmem),
    )(gamma_occ, gamma_pair)
    halves = jnp.swapaxes(gamma_occ.reshape(112, 2, 2, 128), 1, 2)
    return halves.reshape(112, 2, 256), gamma_pair.reshape(448, 1, 512)


def solution(mesh):
    placed = (P(("vb", "oj"), None, "va"), P(("va", "oj"), None, "vb"), P(), P("oj"), P())
    return jax.shard_map(
        per_device,
        mesh=mesh,
        in_specs=placed,
        out_specs=(P(("vb", "oj"), None, "va"), P("va", "oj", "vb")),
        check_vma=False,
    )
```
